128 devices in a mesh: dp: 16 (over z, y), expert: 8 (over x, core).
Axes of the slice: x: 4, y: 4, z: 4, core: 2. Of those that a mesh axis runs over, the one named last changes fastest.
Arguments:
- residual: bfloat16 [8192, 5120], P('dp', 'expert'), may hold values from -36 to 36
- queries: bfloat16 [8192, 5120], P('dp', 'expert'), may hold values from -6 to 6
- keys: bfloat16 [8192, 1024], P('dp', 'expert'), may hold values from -6 to 6
- values: bfloat16 [8192, 1024], P('dp', 'expert'), may hold values from -6 to 6
- lengths: int32 [16, 8], replicated, may hold values from 2 to 256, as said below
- w_out: bfloat16 [5120, 5120], P('expert'), may hold values from -0.125 to 0.125
- w_router: bfloat16 [5120, 16], replicated, may hold values from -0.078125 to 0.078125
- expert_ids: int32 [8192], P('dp'), may hold values from 0 to 15, as said below
- w_gate: bfloat16 [16, 5120, 4096], P('dp', None, 'expert'), may hold values from -0.078125 to 0.078125
- w_up: bfloat16 [16, 5120, 4096], P('dp', None, 'expert'), may hold values from -0.078125 to 0.078125
- w_down: bfloat16 [16, 4096, 5120], P('dp', 'expert'), may hold values from -0.5 to 0.5
Outputs:
- attended: bfloat16 [8192, 5120], P('dp', 'expert')
- expert_out: bfloat16 [8192, 5120], P('dp', 'expert')
The draws below stay inside these ranges and needn't reach their ends.
Inputs may be any that keep to these rules, and one draw needn't show every extreme that they name: `lengths`: each row sums to 512; every document has 2 or more tokens, and each row has one document of exactly 256 tokens. `expert_ids`: within each sequence of 512 tokens no expert is chosen by more than 48 tokens; in every draw one expert is chosen by exactly 48 tokens of every sequence.
All inputs are finite; a program needn't handle non-finite values.
Results may differ from the reference program's by a relative error of at most 0.038.
Values may be sent and summed in bfloat16 or wider, within the bound.
No kernel may reach another device: no remote copies, remote signals or barrier semaphores. Data moves between devices by JAX's collectives and lax.ppermute only.
A program may use at most 128 MiB of HBM per device.

```python
import math
import jax
import jax.numpy as jnp
from jax import lax

D = 5120
H = 40
KVH = 8
HD = 128
EXP_FF = 4096
NDOC = 8
SEQ = 512
EXPERTS = 16
TOKENS = 8192
MAXDOC = 256
CAP = 48
N_EXPERT = 8


def draw_residual(key, part):
    noise_key, scale_key = jax.random.split(jax.random.fold_in(key, 3))
    row_scale = jnp.exp(jax.random.uniform(scale_key, (TOKENS, 1), jnp.float32, math.log(0.3), math.log(3.0)))
    column = jnp.arange(D, dtype=jnp.float32) / D
    noise = jnp.clip(jax.random.normal(noise_key, (TOKENS, D), jnp.float32), -4.0, 4.0)
    column_scale = 0.3 * jnp.power(10.0, column)
    return (noise * row_scale * column_scale[None, :]).astype(jnp.bfloat16)


def draw_queries(key, part):
    noise_key = jax.random.fold_in(key, 1)
    noise = jnp.clip(jax.random.normal(noise_key, (TOKENS, H * HD), jnp.float32), -6.0, 6.0)
    return noise.astype(jnp.bfloat16)


def draw_keys(key, part):
    noise_key = jax.random.fold_in(key, 2)
    noise = jnp.clip(jax.random.normal(noise_key, (TOKENS, KVH * HD), jnp.float32), -6.0, 6.0)
    return noise.astype(jnp.bfloat16)


def draw_lengths(key, part):
    seq_count = TOKENS // SEQ

    def one_row(row_key):
        pick_key, weight_key = jax.random.split(row_key)
        longest = jax.random.randint(pick_key, (), 0, NDOC)
        doc_slots = jnp.arange(NDOC)
        raw_weights = jax.random.randint(weight_key, (NDOC,), 1, 100)
        raw_weights = jnp.where(doc_slots == longest, 0, raw_weights)
        spare_tokens = SEQ - MAXDOC - 2 * (NDOC - 1)
        shares = spare_tokens * raw_weights // jnp.sum(raw_weights)
        leftover = spare_tokens - jnp.sum(shares)
        first_other = jnp.where(longest == 0, 1, 0)
        shares = shares + jnp.where(doc_slots == first_other, leftover, 0)
        return jnp.where(doc_slots == longest, MAXDOC, 2 + shares).astype(jnp.int32)
    return jax.vmap(one_row)(jax.random.split(jax.random.fold_in(key, 5), seq_count))


def draw_expert_ids(key, part):
    seq_count = TOKENS // SEQ
    busy_key, rest_key = jax.random.split(jax.random.fold_in(key, 11))
    busiest = jax.random.randint(busy_key, (), 0, EXPERTS)
    pool_index = jnp.arange((EXPERTS - 1) * CAP)
    others = pool_index // CAP
    others = (others + (others >= busiest).astype(jnp.int32)).astype(jnp.int32)

    def one_seq(seq_key):
        pool_key, order_key = jax.random.split(seq_key)
        picked = jax.random.permutation(pool_key, others)[:SEQ - CAP]
        filled = jnp.concatenate([jnp.zeros((CAP,), jnp.int32) + busiest, picked])
        return jax.random.permutation(order_key, filled)
    return jax.vmap(one_seq)(jax.random.split(rest_key, seq_count)).reshape(TOKENS).astype(jnp.int32)


def with_spikes(drawn, own_key, source, target, blocks, factor):
    def block_of(position):
        return (jnp.arange(drawn.shape[position]) // (drawn.shape[position] // blocks)).reshape((-1,) + (1,) * (drawn.ndim - 1 - position))

    one_side = jax.random.permutation(own_key, blocks)[block_of(target)]
    far = (block_of(target) + blocks // 2) % blocks
    return jnp.where((block_of(source) == one_side) | (block_of(source) == far), factor * drawn, drawn)


def steps_of(rng, extent, pieces, least, top_value):
    factor_of = 1.0
    for dim, parts in pieces:
        steps = jax.random.uniform(jax.random.fold_in(jax.random.fold_in(rng, 6), dim), (parts,), jnp.float32, least / len(pieces), top_value / len(pieces))
        factor_of = factor_of * jnp.repeat(jnp.exp(steps), extent[dim] // parts).reshape((-1,) + (1,) * (len(extent) - 1 - dim))
    return factor_of


def normal_values(own_key, shape, scale, most, cuts=(), kind=jnp.bfloat16):
    loudness = steps_of(own_key, shape, cuts, -0.22, 0.18) if cuts else 1.0
    values = jax.random.normal(own_key, shape, jnp.float32) * scale * loudness
    return jnp.minimum(jnp.maximum(values, -most), most).astype(kind)


def heavy_noise(key, extent, deviation, reach, cuts, heavy, kind=jnp.bfloat16):
    values = deviation * jax.random.normal(key, extent, jnp.float32)
    if cuts:
        values = values * steps_of(key, extent, cuts, -0.22, 0.18)
    return jnp.clip(with_spikes(values, jax.random.fold_in(key, 3), *heavy), -reach, reach).astype(kind)


def setup_inputs(seed: int = 0) -> dict:
    arg_keys = jax.random.split(jax.random.key(seed), 12)
    residual = draw_residual(jax.random.fold_in(arg_keys[11], 71), 0)
    queries = draw_queries(jax.random.fold_in(arg_keys[11], 71), 0)
    keys = draw_keys(jax.random.fold_in(arg_keys[11], 71), 0)
    values = normal_values(arg_keys[3], (TOKENS, KVH * HD), 1.0, 6.0, ((0, 16), (1, 8)))
    lengths = draw_lengths(jax.random.fold_in(arg_keys[11], 71), 0)
    w_out = heavy_noise(arg_keys[5], (H * HD, D), (H * HD) ** -0.5, 0.125, ((0, 8),), (0, 1, 8, 2.0))
    w_router = normal_values(arg_keys[6], (D, EXPERTS), D ** -0.5, 0.078125)
    expert_ids = draw_expert_ids(jax.random.fold_in(arg_keys[11], 71), 0)
    w_gate = normal_values(arg_keys[8], (EXPERTS, D, EXP_FF), D ** -0.5, 0.078125, ((0, 16), (2, 8)))
    w_up = normal_values(arg_keys[9], (EXPERTS, D, EXP_FF), D ** -0.5, 0.078125, ((0, 16), (2, 8)))
    w_down = heavy_noise(arg_keys[10], (EXPERTS, EXP_FF, D), (EXP_FF // 16) ** -0.5, 0.5, ((0, 16), (1, 8)), (1, 2, 8, 2.0))
    return {"residual": residual, "queries": queries, "keys": keys, "values": values, "lengths": lengths, "w_out": w_out, "w_router": w_router, "expert_ids": expert_ids, "w_gate": w_gate, "w_up": w_up, "w_down": w_down}


epsilon = 1e-05

def doc_ids(length_row, positions):
    bounds = jnp.cumsum(length_row)
    return lax.optimization_barrier(jnp.sum((positions[:, None] >= bounds[None, :]).astype(jnp.int32), axis=1))

def attend_sequence(packed):
    seq_queries, seq_keys, seq_values, length_row = packed
    group_size = H // KVH
    positions = jnp.arange(SEQ, dtype=jnp.int32)
    documents = doc_ids(length_row, positions)
    allowed = (documents[:, None] == documents[None, :]) & (positions[None, :] <= positions[:, None])
    shaped_q = seq_queries.astype(jnp.float32).reshape(SEQ, KVH, group_size, HD)
    shaped_k = seq_keys.astype(jnp.float32).reshape(SEQ, KVH, HD)
    shaped_v = seq_values.astype(jnp.float32).reshape(SEQ, KVH, HD)
    scores = jnp.einsum('qkgd,skd->kgqs', shaped_q, shaped_k) / math.sqrt(HD)
    masked = jnp.where(allowed[None, None], scores, -1e+30)
    row_max = lax.optimization_barrier(jnp.max(masked, axis=-1, keepdims=True))
    raised = jnp.exp(masked - row_max)
    weights = (raised / lax.optimization_barrier(jnp.sum(raised, axis=-1, keepdims=True))).astype(jnp.bfloat16)
    mixture = jnp.einsum('kgqs,skd->qkgd', weights.astype(jnp.float32), shaped_v)
    return mixture.astype(jnp.bfloat16).reshape(SEQ, H * HD)

def reference(residual, queries, keys, values, lengths, w_out, w_router, expert_ids, w_gate, w_up, w_down):
    seq_count = TOKENS // SEQ
    context = lax.map(attend_sequence, (queries.reshape(seq_count, SEQ, H * HD), keys.reshape(seq_count, SEQ, KVH * HD), values.reshape(seq_count, SEQ, KVH * HD), lengths))
    context = context.reshape(TOKENS, H * HD)
    head_width = H * HD // N_EXPERT
    slice_width = D // N_EXPERT
    summed = jnp.zeros((TOKENS, D), jnp.float32)
    for member in range(N_EXPERT):
        projected = jnp.dot(context[:, member * head_width:(member + 1) * head_width], w_out[member * head_width:(member + 1) * head_width], preferred_element_type=jnp.float32)
        projected = projected.at[:, member * slice_width:(member + 1) * slice_width].add(residual[:, member * slice_width:(member + 1) * slice_width].astype(jnp.float32))
        rounded = lax.optimization_barrier(projected.astype(jnp.bfloat16))
        summed = summed + rounded.astype(jnp.float32)
    attended = summed.astype(jnp.bfloat16)
    stream = attended.astype(jnp.float32)
    inverse_rms = lax.rsqrt(lax.optimization_barrier(jnp.mean(stream * stream, axis=1, keepdims=True)) + epsilon)
    normed = (stream * inverse_rms).astype(jnp.bfloat16)
    logits = jnp.dot(normed, w_router, preferred_element_type=jnp.float32)
    matches = expert_ids[:, None] == jnp.arange(EXPERTS, dtype=jnp.int32)[None, :]
    chosen = lax.optimization_barrier(jnp.sum(jnp.where(matches, logits, 0.0), axis=1))
    routed = (normed.astype(jnp.float32) * jax.nn.sigmoid(chosen)[:, None]).astype(jnp.bfloat16)
    expert_room = CAP * seq_count
    unit_width = EXP_FF // N_EXPERT

    def run_expert(expert_index):
        token_rows = jnp.nonzero(expert_ids == expert_index, size=expert_room, fill_value=TOKENS)[0].astype(jnp.int32)
        inputs = routed[jnp.minimum(token_rows, TOKENS - 1)]
        gate_part = jnp.dot(inputs, w_gate[expert_index], preferred_element_type=jnp.float32)
        up_part = jnp.dot(inputs, w_up[expert_index], preferred_element_type=jnp.float32)
        hidden = (jax.nn.silu(gate_part) * up_part).astype(jnp.bfloat16)
        down_rows = w_down[expert_index]
        summed_out = jnp.zeros((expert_room, D), jnp.float32)
        for member in range(N_EXPERT):
            projected = jnp.dot(hidden[:, member * unit_width:(member + 1) * unit_width], down_rows[member * unit_width:(member + 1) * unit_width], preferred_element_type=jnp.float32)
            summed_out = summed_out + lax.optimization_barrier(projected.astype(jnp.bfloat16)).astype(jnp.float32)
        return (summed_out.astype(jnp.bfloat16), token_rows)
    outputs, rows_used = lax.map(run_expert, jnp.arange(EXPERTS, dtype=jnp.int32))
    expert_out = jnp.zeros((TOKENS + 1, D), jnp.bfloat16).at[rows_used.reshape(-1)].set(outputs.reshape(-1, D))[:TOKENS]
    return (attended, expert_out)
```

```python
import functools
import math

import jax
import jax.numpy as jnp
from jax import lax
from jax.experimental import pallas as pl
from jax.experimental.pallas import tpu as pltpu
from jax.sharding import Mesh, PartitionSpec as P

HD = 128
EPSILON = 1e-05
PARTS = 2
BF16 = jnp.bfloat16
F32 = jnp.float32
PARAMS = pltpu.CompilerParams(vmem_limit_bytes=28 * 1024 * 1024)


def attend_kernel(first, lengths_ref, q_ref, k_ref, v_ref, out_ref):
    rows, head_width = q_ref.shape
    span = k_ref.shape[0]
    sequence = lax.axis_index("dp")
    row_at = lax.broadcasted_iota(jnp.int32, (rows, 1), 0) + first
    col_at = lax.broadcasted_iota(jnp.int32, (1, span), 1)
    bound = jnp.int32(0)
    row_doc = jnp.zeros((rows, 1), jnp.int32)
    col_doc = jnp.zeros((1, span), jnp.int32)
    for i in range(lengths_ref.shape[1]):
        bound = bound + lengths_ref[sequence, i]
        row_doc = row_doc + (row_at >= bound).astype(jnp.int32)
        col_doc = col_doc + (col_at >= bound).astype(jnp.int32)
    allowed = (row_doc == col_doc) & (col_at <= row_at)
    keys = k_ref[...]
    values = v_ref[...]
    for h in range(head_width // HD):
        cols = slice(h * HD, (h + 1) * HD)
        scores = lax.dot_general(
            q_ref[:, cols], keys, (((1,), (1,)), ((), ())), preferred_element_type=F32
        ) / math.sqrt(HD)
        scores = jnp.where(allowed, scores, -1e30)
        raised = jnp.exp(scores - jnp.max(scores, axis=1, keepdims=True))
        weights = (raised / jnp.sum(raised, axis=1, keepdims=True)).astype(BF16)
        out_ref[:, cols] = jnp.dot(weights, values, preferred_element_type=F32).astype(BF16)


def attend(lengths, queries, keys, values, first, rows):
    span = first + rows
    width = queries.shape[1]
    part = first // rows
    return pl.pallas_call(
        functools.partial(attend_kernel, first),
        grid=(1,),
        out_shape=jax.ShapeDtypeStruct((rows, width), BF16),
        in_specs=[
            pl.BlockSpec(memory_space=pltpu.SMEM),
            pl.BlockSpec((rows, width), lambda i: (part, 0)),
            pl.BlockSpec((span, HD), lambda i: (0, 0)),
            pl.BlockSpec((span, HD), lambda i: (0, 0)),
        ],
        out_specs=pl.BlockSpec((rows, width), lambda i: (0, 0)),
        compiler_params=PARAMS,
        name="attend",
    )(lengths, queries, keys, values)


def pair_kernel(order_ref, x_ref, wc_ref, wo_ref, c_ref, o_ref):
    x = x_ref[...]
    o_ref[...] = jnp.dot(x, wo_ref[...], preferred_element_type=F32).astype(BF16)
    c_ref[...] = jnp.dot(x, wc_ref[...], preferred_element_type=F32).astype(BF16)


def pair_residual_kernel(order_ref, x_ref, wc_ref, wo_ref, r_ref, c_ref, o_ref):
    x = x_ref[...]
    o_ref[...] = jnp.dot(x, wo_ref[...], preferred_element_type=F32).astype(BF16)
    own = jnp.dot(x, wc_ref[...], preferred_element_type=F32) + r_ref[...].astype(F32)
    c_ref[...] = own.astype(BF16)


def pair(x, w, order, width, residual=None, part=0):
    rows, depth = x.shape
    extra = [] if residual is None else [residual]
    specs = [] if residual is None else [pl.BlockSpec((rows, width), lambda i, o: (part, 0))]
    body = pair_kernel if residual is None else pair_residual_kernel
    return pl.pallas_call(
        body,
        grid_spec=pltpu.PrefetchScalarGridSpec(
            num_scalar_prefetch=1,
            grid=(1,),
            in_specs=[
                pl.BlockSpec((rows, depth), lambda i, o: (0, 0)),
                pl.BlockSpec((depth, width), lambda i, o: (0, o[0])),
                pl.BlockSpec((depth, width), lambda i, o: (0, o[1])),
            ]
            + specs,
            out_specs=[pl.BlockSpec((rows, width), lambda i, o: (0, 0))] * 2,
        ),
        out_shape=[jax.ShapeDtypeStruct((rows, width), BF16)] * 2,
        cost_estimate=pl.CostEstimate(
            flops=4 * rows * depth * width,
            bytes_accessed=2 * (rows * depth + 2 * depth * width + 2 * rows * width),
            transcendentals=0,
        ),
        compiler_params=PARAMS,
        name="pair",
    )(order, x, w, w, *extra)


def hidden_kernel(order_ref, *refs):
    count = (len(refs) - 8) + 0
    x_refs = refs[:count]
    wg_ref, wu_ref, wr_ref, out_ref, gate_acc, up_acc, square_acc, logit_acc = refs[count:]
    step = pl.program_id(0)
    for i in range(count):

        @pl.when(step == i)
        def _():
            x = x_refs[i][...]
            wide = x.astype(F32)
            squares = jnp.sum(wide * wide, axis=1, keepdims=True)
            logits = jnp.sum(wide * wr_ref[0], axis=1, keepdims=True)
            gate = jnp.dot(x, wg_ref[...], preferred_element_type=F32)
            up = jnp.dot(x, wu_ref[...], preferred_element_type=F32)
            if i == 0:
                gate_acc[...] = gate
                up_acc[...] = up
                square_acc[...] = squares
                logit_acc[...] = logits
            elif i < count - 1:
                gate_acc[...] += gate
                up_acc[...] += up
                square_acc[...] += squares
                logit_acc[...] += logits
            else:
                features = count * x.shape[1]
                inverse = lax.rsqrt((square_acc[...] + squares) / features + EPSILON)
                logit = (logit_acc[...] + logits) * inverse
                scale = inverse / (1.0 + jnp.exp(-logit))
                gate = (gate_acc[...] + gate) * scale
                up = (up_acc[...] + up) * scale
                out_ref[...] = (gate / (1.0 + jnp.exp(-gate)) * up).astype(BF16)


def hidden_units(shards, w_gate, w_up, router_row, order):
    count = len(shards)
    rows, width = shards[0].shape
    units = w_gate.shape[1]
    return pl.pallas_call(
        hidden_kernel,
        grid_spec=pltpu.PrefetchScalarGridSpec(
            num_scalar_prefetch=1,
            grid=(count,),
            in_specs=[pl.BlockSpec((rows, width), lambda i, o: (0, 0))] * count
            + [
                pl.BlockSpec((width, units), lambda i, o: (o[i], 0)),
                pl.BlockSpec((width, units), lambda i, o: (o[i], 0)),
                pl.BlockSpec((1, 1, width), lambda i, o: (o[i], 0, 0)),
            ],
            out_specs=pl.BlockSpec((rows, units), lambda i, o: (0, 0)),
            scratch_shapes=[
                pltpu.VMEM((rows, units), F32),
                pltpu.VMEM((rows, units), F32),
                pltpu.VMEM((rows, 1), F32),
                pltpu.VMEM((rows, 1), F32),
            ],
        ),
        out_shape=jax.ShapeDtypeStruct((rows, units), BF16),
        cost_estimate=pl.CostEstimate(
            flops=4 * rows * units * width * count,
            bytes_accessed=2 * count * (rows * width + 2 * width * units),
            transcendentals=rows * units,
        ),
        compiler_params=PARAMS,
        name="hidden",
    )(order, *shards, w_gate, w_up, router_row)


def swap(x):
    return lax.ppermute(x, "c", [(0, 1), (1, 0)])


def shift(x, by):
    size = lax.axis_size("x")
    return lax.ppermute(x, "x", [(i, (i + by) % size) for i in range(size)])


def total(*terms):
    return sum(t.astype(F32) for t in terms).astype(BF16)


def reduce_parts(make, by):
    far, far_other = make(2)
    far = shift(total(far, swap(far_other)), by)
    near, near_other = make(-by)
    near = shift(total(near, swap(near_other)), -by)
    next_, next_other = make(by)
    next_ = shift(total(next_, swap(next_other), far), by)
    own, own_other = make(0)
    return total(own, swap(own_other), near, next_)


def gather_parts(x, by):
    behind = shift(x, by)
    ahead = shift(x, -by)
    far = shift(behind, by)
    return [x, swap(x), behind, swap(behind), ahead, swap(ahead), far, swap(far)]


def shards(
    residual, queries, keys, values, lengths, w_out, w_router, expert_ids, w_gate, w_up, w_down
):
    seq_len = queries.shape[0]
    width = residual.shape[1]
    dp_count = lax.axis_size("dp")
    x_count = lax.axis_size("x")
    x_index = lax.axis_index("x")
    core = lax.axis_index("c")
    expert_count = w_router.shape[1]
    capacity = 3 * seq_len // (2 * expert_count)
    share = capacity // PARTS

    def blocks_at(by):
        base = 2 * ((x_index + by) % x_count)
        return jnp.stack([base + core, base + 1 - core]).astype(jnp.int32)

    at = {k: blocks_at(k) for k in (0, 1, 2, -1)}

    rows = seq_len // PARTS
    attended = []
    for part in range(PARTS):
        by = 1 if part % 2 == 0 else -1
        context = attend(lengths, queries, keys, values, part * rows, rows)

        def project(k):
            if k == 0:
                return pair(context, w_out, at[0], width, residual, part)
            return pair(context, w_out, at[k], width)

        attended.append(reduce_parts(project, by))
    attended = jnp.concatenate(attended, axis=0)

    same = expert_ids[:, None] == expert_ids[None, :]
    token_at = jnp.arange(seq_len, dtype=jnp.int32)
    rank = jnp.sum((same & (token_at[None, :] < token_at[:, None])).astype(jnp.int32), axis=1)
    slot = (rank // share) * (expert_count * share) + expert_ids * share + rank % share
    part_slots = expert_count * share
    router_row = lax.dynamic_index_in_dim(
        w_router.astype(F32).T, lax.axis_index("dp"), 0, keepdims=False
    ).reshape(2 * x_count, 1, width)
    gate_w, up_w, down_w = w_gate[0], w_up[0], w_down[0]

    expert_out = None
    arrived = []
    picks = []
    for part in range(PARTS):
        slots = jnp.arange(part * part_slots, (part + 1) * part_slots, dtype=jnp.int32)
        pick = (slots[:, None] == slot[None, :]).astype(BF16)
        picks.append(pick)
        outgoing = jnp.dot(pick, attended, preferred_element_type=F32).astype(BF16)
        outgoing = outgoing.reshape(dp_count, part_slots // dp_count, width)
        arrived.append(
            lax.all_to_all(outgoing, "dp", split_axis=0, concat_axis=0, tiled=True).reshape(
                part_slots, width
            )
        )
    summed = []
    for part in range(PARTS):
        by = 1 if part % 2 == 0 else -1
        every = gather_parts(arrived[part], by)
        order = jnp.concatenate([at[0], at[-by], at[by], at[2]])
        hidden = hidden_units(every, gate_w, up_w, router_row, order)
        summed.append(reduce_parts(lambda k: pair(hidden, down_w, at[k], width), by))
    expert_out = 0.0
    for part in range(PARTS):
        back = summed[part].reshape(dp_count, part_slots // dp_count, width)
        back = lax.all_to_all(back, "dp", split_axis=0, concat_axis=0, tiled=True)
        expert_out = expert_out + lax.dot_general(
            picks[part],
            back.reshape(part_slots, width),
            (((0,), (0,)), ((), ())),
            preferred_element_type=F32,
        )
    return (attended, expert_out.astype(BF16))


def solution(mesh):
    chips = mesh.shape["expert"] // 2
    fine = Mesh(mesh.devices.reshape(mesh.shape["dp"], chips, 2), ("dp", "x", "c"))
    e = ("x", "c")
    in_specs = (
        P("dp", e),
        P("dp", e),
        P("dp", e),
        P("dp", e),
        P(),
        P(e, None),
        P(),
        P("dp"),
        P("dp", None, e),
        P("dp", None, e),
        P("dp", e, None),
    )
    out_specs = (P("dp", e), P("dp", e))
    return jax.shard_map(shards, mesh=fine, in_specs=in_specs, out_specs=out_specs, check_vma=False)
```

```python
import functools
import math

import jax
import jax.numpy as jnp
from jax import lax
from jax.experimental import pallas as pl
from jax.experimental.pallas import tpu as pltpu
from jax.sharding import Mesh, PartitionSpec as P

HD = 128
EPSILON = 1e-05
BF16 = jnp.bfloat16
F32 = jnp.float32
ANY = pl.BlockSpec(memory_space=pl.ANY)
VMEM = pl.BlockSpec(memory_space=pltpu.VMEM)


def params(mib=20):
    return pltpu.CompilerParams(vmem_limit_bytes=mib * 1024 * 1024)


HOPS = (2, 1, -1, 0)
TOKEN = jax.ShapeDtypeStruct((8, 128), F32)


def chip_at(hop):
    return lax.rem(lax.axis_index("x") + hop + 4, 4)


def column_copies(w_ref, targets, others, sems):
    core = lax.axis_index("c")
    width = targets[0].shape[1]
    copies = []
    for k, (hop, target) in enumerate(zip(HOPS, targets)):
        start = pl.multiple_of((2 * chip_at(hop) + (1 - core if others else core)) * width, 128)
        copy = pltpu.make_async_copy(w_ref.at[:, pl.ds(start, width)], target, sems.at[k])
        copy.start()
        copies.append(copy)
    return copies


def column_shape(w, width, n):
    return jax.ShapeDtypeStruct((n, w.shape[0], width), BF16)


def columns_kernel(w_ref, own_ref, far_ref, rest_ref, token_ref, sems, other_sems):
    token_ref[...] = jnp.zeros_like(token_ref)
    count = len(HOPS)
    others = [far_ref.at[0]] + [rest_ref.at[k] for k in range(count - 1)]
    copies = column_copies(w_ref, others, True, other_sems)
    copies += column_copies(w_ref, [own_ref.at[k] for k in range(count)], False, sems)
    for copy in copies:
        copy.wait()


def columns(w, width):
    count = len(HOPS)
    return pl.pallas_call(
        columns_kernel,
        in_specs=[ANY],
        out_specs=[VMEM] * 4,
        out_shape=[column_shape(w, width, n) for n in (count, 1, count - 1)] + [TOKEN],
        scratch_shapes=[pltpu.SemaphoreType.DMA((count,)), pltpu.SemaphoreType.DMA((count,))],
        compiler_params=params(52),
        name="columns",
    )(w)


def attend_kernel(halves, lengths_ref, q_ref, k_ref, v_ref, after_ref, out_ref):
    seq_len, head_width = q_ref.shape
    rows = seq_len // halves
    sequence = lax.axis_index("dp")
    for part in range(halves):
        first = part * rows
        span = first + rows
        row_at = lax.broadcasted_iota(jnp.int32, (rows, 1), 0) + first
        col_at = lax.broadcasted_iota(jnp.int32, (1, span), 1)
        bound = jnp.int32(0)
        row_doc = jnp.zeros((rows, 1), jnp.int32)
        col_doc = jnp.zeros((1, span), jnp.int32)
        for i in range(lengths_ref.shape[0]):
            bound = bound + lengths_ref[i, sequence]
            row_doc = row_doc + (row_at >= bound).astype(jnp.int32)
            col_doc = col_doc + (col_at >= bound).astype(jnp.int32)
        allowed = (row_doc == col_doc) & (col_at <= row_at)
        keys = k_ref[:span, :]
        values = v_ref[:span, :]
        for h in range(head_width // HD):
            cols = slice(h * HD, (h + 1) * HD)
            scores = lax.dot_general(
                q_ref[first:span, cols],
                keys,
                (((1,), (1,)), ((), ())),
                preferred_element_type=F32,
            ) * (1.0 / math.sqrt(HD))
            scores = jnp.where(allowed, scores, -1e30)
            raised = jnp.exp(scores - jnp.max(scores, axis=1, keepdims=True))
            share = 1.0 / jnp.sum(raised, axis=1, keepdims=True)
            mixed = jnp.dot((raised * share).astype(BF16), values, preferred_element_type=F32)
            out_ref[first:span, cols] = mixed.astype(BF16)


def attend(lengths, queries, keys, values, after):
    return pl.pallas_call(
        functools.partial(attend_kernel, 2),
        out_shape=jax.ShapeDtypeStruct(queries.shape, BF16),
        in_specs=[pl.BlockSpec(memory_space=pltpu.SMEM), VMEM, VMEM, VMEM, ANY],
        out_specs=VMEM,
        compiler_params=params(),
        name="attend",
    )(lengths.T, queries, keys, values, after)


def weights_kernel(count, hops, down_ref, gate_ref, up_ref, *refs):
    own_ref, other_ref, g_ref, u_ref, token_ref, sems, other_sems, row_sems = refs[count:]
    token_ref[...] = jnp.zeros_like(token_ref)
    copies = []
    for target, others, used in ((other_ref, True, other_sems), (own_ref, False, sems)):
        copies += column_copies(down_ref, [target.at[k] for k in range(len(HOPS))], others, used)
    core = lax.axis_index("c")
    width = own_ref.shape[2]
    for k, hop in enumerate(hops):
        for j, place in enumerate((core, 1 - core)):
            start = pl.multiple_of((2 * chip_at(hop) + place) * width, 128)
            target = pl.ds((2 * k + j) * width, width)
            for i, (source, buffer) in enumerate(((gate_ref, g_ref), (up_ref, u_ref))):
                copy = pltpu.make_async_copy(
                    source.at[pl.ds(start, width), :], buffer.at[target, :], row_sems.at[4 * k + 2 * j + i]
                )
                copy.start()
                copies.append(copy)
    for copy in copies:
        copy.wait()


def expert_weights(down, gate, up, width, hops, after):
    rows = jax.ShapeDtypeStruct(gate.shape, BF16)
    return pl.pallas_call(
        functools.partial(weights_kernel, len(after), hops),
        in_specs=[ANY] * 3 + [ANY] * len(after),
        out_specs=[VMEM] * 5,
        out_shape=[column_shape(down, width, len(HOPS))] * 2 + [rows, rows, TOKEN],
        scratch_shapes=[
            pltpu.SemaphoreType.DMA((len(HOPS),)),
            pltpu.SemaphoreType.DMA((len(HOPS),)),
            pltpu.SemaphoreType.DMA((4 * len(hops),)),
        ],
        compiler_params=params(43),
        name="expert_weights",
    )(down, gate, up, *after)


def far_kernel(x_ref, xs_ref, w_ref, ws_ref, up_ref, low_ref):
    half = up_ref.shape[0]
    value = jnp.dot(x_ref[...], w_ref[0], preferred_element_type=F32)
    value = value + jnp.dot(xs_ref[...], ws_ref[0], preferred_element_type=F32)
    up_ref[...] = value[:half].astype(BF16)
    low_ref[...] = value[half:].astype(BF16)


def near_kernel(shared, x_ref, xs_ref, w_ref, ws_ref, after_ref, near_low, near_up, next_up, next_low, own_ref):
    half = near_up.shape[0]
    x, xs = x_ref[...], xs_ref[...]

    def product(k):
        value = jnp.dot(x, w_ref[k], preferred_element_type=F32)
        return value + jnp.dot(xs, ws_ref[k if shared else k - 1], preferred_element_type=F32)

    value = product(1)
    next_up[...] = value[:half]
    near_low[...] = value[half:].astype(BF16)
    value = product(2)
    near_up[...] = value[:half].astype(BF16)
    next_low[...] = value[half:]
    own_ref[...] = product(3)


def next_kernel(next_up, next_low, far_up, far_low, up_ref, low_ref):
    up_ref[...] = (next_up[...] + far_up[...].astype(F32)).astype(BF16)
    low_ref[...] = (next_low[...] + far_low[...].astype(F32)).astype(BF16)


def own_kernel(attention, count, own_ref, *refs):
    arrived = refs[:4]
    half = arrived[0].shape[0]
    for lower in range(2):
        rows = slice(lower * half, (lower + 1) * half)
        value = own_ref[rows, :]
        for ref in arrived[2 * lower : 2 * lower + 2]:
            value = value + ref[...].astype(F32)
        if attention:
            residual_ref, slot_ref = refs[4:6]
            out_ref, slots_ref = refs[6 + count :]
            value = value + residual_ref[rows, :].astype(F32)
        else:
            out_ref = refs[4 + count]
        out_ref[rows, :] = value.astype(BF16)
    if attention:
        places = lax.broadcasted_iota(jnp.int32, (slots_ref.shape[0], 1), 0)
        pick = (places == slot_ref[...]).astype(F32).astype(BF16)
        slots_ref[...] = jnp.dot(pick, out_ref[...], preferred_element_type=F32).astype(BF16)


def call(kernel, inputs, outs, name, after=(), flops=0):
    return pl.pallas_call(
        kernel,
        in_specs=[VMEM] * len(inputs) + [ANY] * len(after),
        out_specs=[VMEM] * len(outs),
        out_shape=[jax.ShapeDtypeStruct(shape, dtype) for shape, dtype in outs],
        cost_estimate=pl.CostEstimate(flops=flops, bytes_accessed=1024, transcendentals=0),
        compiler_params=params(),
        name=name,
    )(*inputs, *after)


def swap(x):
    return lax.ppermute(x, "c", [(0, 1), (1, 0)])


def shift(x, by):
    size = lax.axis_size("x")
    return lax.ppermute(x, "x", [(i, (i + by) % size) for i in range(size)])


def reduce_blocks(x, w, far_w, rest_w, attention=(), slots=None, middle=None):
    xs = swap(x)
    rows, depth = x.shape
    width = far_w.shape[2]
    half = ((rows // 2, width), BF16)
    half_f32 = ((rows // 2, width), F32)
    flops = 4 * rows * depth * width
    far = call(far_kernel, (x, xs, w, far_w), [half] * 2, "far_blocks", flops=flops)
    far_up, far_low = shift(far[0], 1), shift(far[1], -1)
    near_low, near_up, next_up, next_low, own = call(
        functools.partial(near_kernel, rest_w is far_w),
        (x, xs, w, rest_w, far[0]),
        [half, half, half_f32, half_f32, ((rows, width), F32)],
        "near_blocks",
        flops=3 * flops,
    )
    near_low, near_up = shift(near_low, 1), shift(near_up, -1)
    last = call(next_kernel, (next_up, next_low, far_up, far_low), [half] * 2, "next_blocks")
    last_up, last_low = shift(last[0], 1), shift(last[1], -1)
    inputs = [own, near_up, last_up, near_low, last_low]
    outs = [((rows, width), BF16)]
    if attention:
        inputs += attention
        outs.append(((slots, width), BF16))
    between = middle(last[0]) if middle else ()
    kernel = functools.partial(own_kernel, bool(attention), len(between[-1:]))
    return call(kernel, inputs, outs, "own_block", between[-1:]), between


def hidden_kernel(begin, end, offset, features, count, *refs):
    x_refs = refs[:count]
    wg_ref, wu_ref, wr_ref = refs[count : count + 3]
    rest = refs[count + 3 :]
    width = x_refs[0].shape[1]
    x = jnp.concatenate([ref[...] for ref in x_refs], axis=1)
    span = slice(offset * width, (offset + count) * width)
    wide = x.astype(F32)
    squares = jnp.sum(wide * wide, axis=1, keepdims=True)
    logits = jnp.sum(wide * wr_ref[:, span], axis=1, keepdims=True)
    gate = jnp.dot(x, wg_ref[span, :], preferred_element_type=F32)
    up = jnp.dot(x, wu_ref[span, :], preferred_element_type=F32)
    if not begin:
        gate, up = rest[0][...] + gate, rest[1][...] + up
        squares, logits = rest[2][...] + squares, rest[3][...] + logits
        rest = rest[4:]
    if not end:
        for ref, value in zip(rest, (gate, up, squares, logits)):
            ref[...] = value
        return
    inverse = lax.rsqrt(squares / features + EPSILON)
    scale = inverse / (1.0 + jnp.exp(-logits * inverse))
    gate = gate * scale
    rest[0][...] = (gate / (1.0 + jnp.exp(-gate)) * (up * scale)).astype(BF16)


def hidden_units(shards, offset, weights, begun=(), end=True):
    rows, width = shards[0].shape
    features, units = weights[0].shape
    outs = [((rows, units), BF16)] if end else [((rows, n), F32) for n in (units, units, 1, 1)]
    kernel = functools.partial(hidden_kernel, not begun, end, offset, features, len(shards))
    flops = 4 * rows * units * width * len(shards)
    return call(kernel, (*shards, *weights, *begun), outs, "hidden", flops=flops)


def halves_kernel(behind_ref, ahead_ref, *refs):
    up_ref, low_ref = refs[-2:]
    half = up_ref.shape[0]
    up_ref[...] = behind_ref[:half, :]
    low_ref[...] = ahead_ref[half:, :]


def join_kernel(up_ref, low_ref, *refs):
    half = up_ref.shape[0]
    refs[-1][:half, :] = up_ref[...]
    refs[-1][half:, :] = low_ref[...]


def from_slots_kernel(slot_ref, x_ref, out_ref):
    places = lax.broadcasted_iota(jnp.int32, (1, x_ref.shape[0]), 1)
    pick = (slot_ref[...] == places).astype(F32).astype(BF16)
    out_ref[...] = jnp.dot(pick, x_ref[...], preferred_element_type=F32).astype(BF16)


def shards(
    residual, queries, keys, values, lengths, w_out, w_router, expert_ids, w_gate, w_up, w_down
):
    seq_len = queries.shape[0]
    width = residual.shape[1]
    dp_count = lax.axis_size("dp")
    x_count = lax.axis_size("x")
    expert_count = w_router.shape[1]
    capacity = 3 * seq_len // (2 * expert_count)
    slots = expert_count * capacity

    same = expert_ids[:, None] == expert_ids[None, :]
    token_at = jnp.arange(seq_len, dtype=jnp.int32)
    rank = jnp.sum((same & (token_at[None, :] < token_at[:, None])).astype(jnp.int32), axis=1)
    slot = expert_ids * capacity + rank

    arrival = (0, -1, 1, 2)
    core = lax.axis_index("c")
    router = lax.dynamic_index_in_dim(w_router.astype(F32).T, lax.axis_index("dp"), 0, keepdims=False)
    router = router.reshape(x_count, 2, width)
    router = jnp.where(core == 0, router, router[:, ::-1])
    chips = (lax.axis_index("x") + jnp.array(arrival) + x_count) % x_count
    router = router[chips].reshape(1, -1)

    w_own, w_far, w_rest, token = columns(w_out, width)
    context = attend(lengths, queries, keys, values, token)

    def meanwhile(done):
        return expert_weights(w_down[0], w_gate[0], w_up[0], width, arrival, (done, router))

    (attended, outgoing), ready = reduce_blocks(
        context, w_own, swap(w_far), swap(w_rest), [residual, slot.reshape(1, -1)], slots, meanwhile
    )
    down_own, down_other, gate, up, _ = ready
    down_other = swap(down_other)

    def exchange(x):
        x = x.reshape(dp_count, slots // dp_count, width)
        return lax.all_to_all(x, "dp", split_axis=0, concat_axis=0, tiled=True).reshape(slots, width)

    here = exchange(outgoing)
    weights = (gate, up, router)
    behind, ahead = shift(here, 1), shift(here, -1)
    half = ((slots // 2, width), BF16)
    behind_up, ahead_low = call(halves_kernel, (behind, ahead), [half] * 2, "halves")
    far_up, far_low = shift(behind_up, 1), shift(ahead_low, -1)
    near = [here, swap(here), behind, swap(behind), ahead, swap(ahead)]
    begun = hidden_units(near, 0, weights, end=False)
    (far,) = call(
        join_kernel, (far_up, far_low), [((slots, width), BF16)], "join", after=(begun[2],)
    )
    (hidden,) = hidden_units([far, swap(far)], 6, weights, begun)
    (summed,), _ = reduce_blocks(hidden, down_own, down_other, down_other)
    (expert_out,) = call(
        lambda s, x, o: from_slots_kernel(s, x, o),
        (slot.reshape(-1, 1), exchange(summed)),
        [((seq_len, width), BF16)],
        "from_slots",
    )
    return (attended, expert_out)


def solution(mesh):
    chips = mesh.shape["expert"] // 2
    fine = Mesh(mesh.devices.reshape(mesh.shape["dp"], chips, 2), ("dp", "x", "c"))
    e = ("x", "c")
    in_specs = (
        P("dp", e),
        P("dp", e),
        P("dp", e),
        P("dp", e),
        P(),
        P(e, None),
        P(),
        P("dp"),
        P("dp", None, e),
        P("dp", None, e),
        P("dp", e, None),
    )
    out_specs = (P("dp", e), P("dp", e))
    return jax.shard_map(shards, mesh=fine, in_specs=in_specs, out_specs=out_specs, check_vma=False)
```

```python
import functools
import math

import jax
import jax.numpy as jnp
from jax import lax
from jax.experimental import pallas as pl
from jax.experimental.pallas import tpu as pltpu
from jax.sharding import Mesh, PartitionSpec as P

HD = 128
EPSILON = 1e-05
BF16 = jnp.bfloat16
F32 = jnp.float32
ANY = pl.BlockSpec(memory_space=pl.ANY)
VMEM = pl.BlockSpec(memory_space=pltpu.VMEM)


def params(mib=20):
    return pltpu.CompilerParams(vmem_limit_bytes=mib * 1024 * 1024)


HOPS = (2, 1, -1, 0)
COST = pl.CostEstimate(flops=1024, bytes_accessed=1024, transcendentals=0)
TOKEN = jax.ShapeDtypeStruct((8, 128), F32)


def chip_at(hop):
    return lax.rem(lax.axis_index("x") + hop + 4, 4)


def column_copies(w_ref, targets, others, sems):
    core = lax.axis_index("c")
    width = targets[0].shape[1]
    copies = []
    for k, (hop, target) in enumerate(zip(HOPS, targets)):
        start = pl.multiple_of((2 * chip_at(hop) + (1 - core if others else core)) * width, 128)
        copy = pltpu.make_async_copy(w_ref.at[:, pl.ds(start, width)], target, sems.at[k])
        copy.start()
        copies.append(copy)
    return copies


def column_shape(w, width, n):
    return jax.ShapeDtypeStruct((n, w.shape[0], width), BF16)


def columns_kernel(w_ref, *refs):
    own_far_ref, own_rest_ref, far_ref, rest_ref, token_ref, sems, other_sems = refs[-7:]
    token_ref[...] = jnp.zeros_like(token_ref)
    copies = []
    for others, first, rest, used in ((True, far_ref, rest_ref, other_sems), (False, own_far_ref, own_rest_ref, sems)):
        targets = [first.at[0]] + [rest.at[k] for k in range(len(HOPS) - 1)]
        copies += column_copies(w_ref, targets, others, used)
    for copy in copies:
        copy.wait()


def columns(w, width, after=()):
    count = len(HOPS)
    return pl.pallas_call(
        columns_kernel,
        in_specs=[ANY] * (1 + len(after)),
        out_specs=[VMEM] * 5,
        out_shape=[column_shape(w, width, n) for n in (1, count - 1, 1, count - 1)] + [TOKEN],
        scratch_shapes=[pltpu.SemaphoreType.DMA((count,)), pltpu.SemaphoreType.DMA((count,))],
        cost_estimate=COST,
        compiler_params=params(),
        name="columns",
    )(w, *after)


def attend_kernel(halves, lengths_ref, q_ref, k_ref, v_ref, after_ref, out_ref):
    seq_len, head_width = q_ref.shape
    rows = seq_len // halves
    sequence = lax.axis_index("dp")
    for part in range(halves):
        first = part * rows
        span = first + rows
        row_at = lax.broadcasted_iota(jnp.int32, (rows, 1), 0) + first
        col_at = lax.broadcasted_iota(jnp.int32, (1, span), 1)
        bound = jnp.int32(0)
        row_doc = jnp.zeros((rows, 1), jnp.int32)
        col_doc = jnp.zeros((1, span), jnp.int32)
        for i in range(lengths_ref.shape[0]):
            bound = bound + lengths_ref[i, sequence]
            row_doc = row_doc + (row_at >= bound).astype(jnp.int32)
            col_doc = col_doc + (col_at >= bound).astype(jnp.int32)
        allowed = (row_doc == col_doc) & (col_at <= row_at)
        keys = k_ref[:span, :]
        values = v_ref[:span, :]
        for h in range(head_width // HD):
            cols = slice(h * HD, (h + 1) * HD)
            scores = lax.dot_general(
                q_ref[first:span, cols],
                keys,
                (((1,), (1,)), ((), ())),
                preferred_element_type=F32,
            ) * (1.0 / math.sqrt(HD))
            scores = jnp.where(allowed, scores, -1e30)
            raised = jnp.exp(scores - jnp.max(scores, axis=1, keepdims=True))
            share = 1.0 / jnp.sum(raised, axis=1, keepdims=True)
            mixed = jnp.dot((raised * share).astype(BF16), values, preferred_element_type=F32)
            out_ref[first:span, cols] = mixed.astype(BF16)


def attend(lengths, queries, keys, values, after):
    return pl.pallas_call(
        functools.partial(attend_kernel, 2),
        out_shape=jax.ShapeDtypeStruct(queries.shape, BF16),
        in_specs=[pl.BlockSpec(memory_space=pltpu.SMEM), VMEM, VMEM, VMEM, VMEM],
        out_specs=VMEM,
        cost_estimate=COST,
        compiler_params=params(),
        name="attend",
    )(lengths.T, queries, keys, values, after)


def far_kernel(x_ref, xs_ref, w_ref, ws_ref, up_ref, low_ref):
    half = up_ref.shape[0]
    value = jnp.dot(x_ref[...], w_ref[0], preferred_element_type=F32)
    value = value + jnp.dot(xs_ref[...], ws_ref[0], preferred_element_type=F32)
    up_ref[...] = value[:half].astype(BF16)
    low_ref[...] = value[half:].astype(BF16)


def near_kernel(x_ref, xs_ref, w_ref, ws_ref, after_ref, near_low, near_up):
    half = near_up.shape[0]
    for k, rows, out_ref in ((1, slice(half, 2 * half), near_low), (2, slice(0, half), near_up)):
        value = jnp.dot(x_ref[rows, :], w_ref[k - 1], preferred_element_type=F32)
        value = value + jnp.dot(xs_ref[rows, :], ws_ref[k - 1], preferred_element_type=F32)
        out_ref[...] = value.astype(BF16)


def rest_kernel(x_ref, xs_ref, w_ref, ws_ref, after_ref, next_up, next_low, own_ref):
    half = next_up.shape[0]
    for k, rows, out_ref in (
        (1, slice(0, half), next_up),
        (2, slice(half, 2 * half), next_low),
        (3, slice(0, 2 * half), own_ref),
    ):
        value = jnp.dot(x_ref[rows, :], w_ref[k - 1], preferred_element_type=F32)
        out_ref[...] = value + jnp.dot(xs_ref[rows, :], ws_ref[k - 1], preferred_element_type=F32)


def next_kernel(next_up, next_low, far_up, far_low, up_ref, low_ref):
    up_ref[...] = (next_up[...] + far_up[...].astype(F32)).astype(BF16)
    low_ref[...] = (next_low[...] + far_low[...].astype(F32)).astype(BF16)


def own_kernel(attention, count, own_ref, *refs):
    arrived = refs[:4]
    half = arrived[0].shape[0]
    for lower in range(2):
        rows = slice(lower * half, (lower + 1) * half)
        value = own_ref[rows, :]
        for ref in arrived[2 * lower : 2 * lower + 2]:
            value = value + ref[...].astype(F32)
        if attention:
            residual_ref, slot_ref = refs[4:6]
            out_ref, slots_ref = refs[6 + count :]
            value = value + residual_ref[rows, :].astype(F32)
        else:
            out_ref = refs[4 + count]
        out_ref[rows, :] = value.astype(BF16)
    if attention:
        places = lax.broadcasted_iota(jnp.int32, (slots_ref.shape[0], 1), 0)
        pick = (places == slot_ref[...]).astype(F32).astype(BF16)
        slots_ref[...] = jnp.dot(pick, out_ref[...], preferred_element_type=F32).astype(BF16)


def call(kernel, inputs, outs, name, after=()):
    return pl.pallas_call(
        kernel,
        in_specs=[VMEM] * len(inputs) + [ANY] * len(after),
        out_specs=[VMEM] * len(outs),
        out_shape=[jax.ShapeDtypeStruct(shape, dtype) for shape, dtype in outs],
        cost_estimate=COST,
        compiler_params=params(),
        name=name,
    )(*inputs, *after)


def swap(x):
    return lax.ppermute(x, "c", [(0, 1), (1, 0)])


def shift(x, by):
    size = lax.axis_size("x")
    return lax.ppermute(x, "x", [(i, (i + by) % size) for i in range(size)])


def reduce_blocks(x, w_far, w_rest, other_far, other_rest, attention=(), slots=None, middle=None):
    xs = swap(x)
    rows, depth = x.shape
    width = w_far.shape[2]
    half = ((rows // 2, width), BF16)
    half_f32 = ((rows // 2, width), F32)
    far = call(far_kernel, (x, xs, w_far, other_far), [half] * 2, "far_blocks")
    far_up, far_low = shift(far[0], 1), shift(far[1], -1)
    near = call(
        near_kernel,
        (x, xs, w_rest, other_rest, far[0]),
        [half] * 2,
        "near_blocks",
    )
    near_low, near_up = shift(near[0], 1), shift(near[1], -1)
    next_up, next_low, own = call(
        rest_kernel,
        (x, xs, w_rest, other_rest, near[0]),
        [half_f32, half_f32, ((rows, width), F32)],
        "rest_blocks",
    )
    last = call(next_kernel, (next_up, next_low, far_up, far_low), [half] * 2, "next_blocks")
    last_up, last_low = shift(last[0], 1), shift(last[1], -1)
    inputs = [own, near_up, last_up, near_low, last_low]
    outs = [((rows, width), BF16)]
    if attention:
        inputs += attention
        outs.append(((slots, width), BF16))
    between = middle(last[0]) if middle else ()
    kernel = functools.partial(own_kernel, bool(attention), len(between[-1:]))
    return call(kernel, inputs, outs, "own_block", between[-1:]), between


def hidden_kernel(hops, begin, end, features, count, *refs):
    shards = 2 * len(hops)
    x_refs = refs[:shards]
    wg_ref, wu_ref, wr_ref = refs[shards : shards + 3]
    rest = refs[shards + 3 :]
    depth = 2 * x_refs[0].shape[1]
    first_core = lax.axis_index("c") == 0
    sums = None
    if not begin:
        sums, rest = [ref[...] for ref in rest[:4]], rest[4:]
    rest = rest[count:]
    for k, hop in enumerate(hops):
        mine, other = x_refs[2 * k][...], x_refs[2 * k + 1][...]
        x = jnp.concatenate(
            [jnp.where(first_core, mine, other), jnp.where(first_core, other, mine)], axis=1
        )
        start = pl.multiple_of(chip_at(hop) * depth, 128)
        at = 0 if hop == 0 else depth
        rows = pl.ds(start, depth) if begin else slice(at, at + depth)
        wide = x.astype(F32)
        terms = (
            jnp.dot(x, wg_ref[rows, :], preferred_element_type=F32),
            jnp.dot(x, wu_ref[rows, :], preferred_element_type=F32),
            jnp.sum(wide * wide, axis=1, keepdims=True),
            jnp.sum(wide * wr_ref[:, pl.ds(start, depth)], axis=1, keepdims=True),
        )
        sums = terms if sums is None else [a + b for a, b in zip(sums, terms)]
    if not end:
        for ref, value in zip(rest, sums):
            ref[...] = value
        if begin:
            for i, hop in enumerate((0, 2)):
                rows = pl.ds(pl.multiple_of(chip_at(hop) * depth, 128), depth)
                rest[4][i * depth : (i + 1) * depth, :] = wg_ref[rows, :]
                rest[5][i * depth : (i + 1) * depth, :] = wu_ref[rows, :]
        return
    gate, up, squares, logits = sums
    inverse = lax.rsqrt(squares / features + EPSILON)
    scale = inverse / (1.0 + jnp.exp(-logits * inverse))
    gate = gate * scale
    rest[0][...] = (gate / (1.0 + jnp.exp(-gate)) * (up * scale)).astype(BF16)


def hidden_units(shards, hops, weights, begun=(), end=False, after=()):
    rows, width = shards[0].shape
    features, units = weights[2].shape[1], weights[0].shape[1]
    if end:
        outs = [((rows, units), BF16)]
    else:
        outs = [((rows, n), F32) for n in (units, units, 1, 1)]
        outs += [] if begun else [((4 * width, units), BF16)] * 2
    kernel = functools.partial(hidden_kernel, hops, not begun, end, features, len(after))
    return call(kernel, (*shards, *weights, *begun), outs, "hidden", after)


def halves_kernel(behind_ref, ahead_ref, up_ref, low_ref):
    half = up_ref.shape[0]
    up_ref[...] = behind_ref[:half, :]
    low_ref[...] = ahead_ref[half:, :]


def join_kernel(up_ref, low_ref, *refs):
    half = up_ref.shape[0]
    refs[-1][:half, :] = up_ref[...]
    refs[-1][half:, :] = low_ref[...]


def from_slots_kernel(slot_ref, x_ref, out_ref):
    places = lax.broadcasted_iota(jnp.int32, (1, x_ref.shape[0]), 1)
    pick = (slot_ref[...] == places).astype(F32).astype(BF16)
    out_ref[...] = jnp.dot(pick, x_ref[...], preferred_element_type=F32).astype(BF16)


def shards(
    residual, queries, keys, values, lengths, w_out, w_router, expert_ids, w_gate, w_up, w_down
):
    seq_len = queries.shape[0]
    width = residual.shape[1]
    dp_count = lax.axis_size("dp")
    expert_count = w_router.shape[1]
    capacity = 3 * seq_len // (2 * expert_count)
    slots = expert_count * capacity

    same = expert_ids[:, None] == expert_ids[None, :]
    token_at = jnp.arange(seq_len, dtype=jnp.int32)
    rank = jnp.sum((same & (token_at[None, :] < token_at[:, None])).astype(jnp.int32), axis=1)
    slot = expert_ids * capacity + rank

    router = lax.dynamic_index_in_dim(w_router.astype(F32).T, lax.axis_index("dp"), 0)

    w_far, w_rest, other_far, other_rest, token = columns(w_out, width)
    context = attend(lengths, queries, keys, values, token)

    (attended, outgoing), (*down, _) = reduce_blocks(
        context,
        w_far,
        w_rest,
        swap(other_far),
        swap(other_rest),
        [residual, slot.reshape(1, -1)],
        slots,
        lambda done: columns(w_down[0], width, (done,)),
    )
    down[2], down[3] = swap(down[2]), swap(down[3])

    def exchange(x):
        x = x.reshape(dp_count, slots // dp_count, width)
        return lax.all_to_all(x, "dp", split_axis=0, concat_axis=0, tiled=True).reshape(slots, width)

    here = exchange(outgoing)
    behind, ahead = shift(here, 1), shift(here, -1)
    half, full = ((slots // 2, width), BF16), ((slots, width), BF16)
    behind_up, ahead_low = call(halves_kernel, (behind, ahead), [half] * 2, "halves")
    far_up, far_low = shift(behind_up, 1), shift(ahead_low, -1)
    beside = [behind, swap(behind), ahead, swap(ahead)]
    *begun, gate, up = hidden_units(beside, (-1, 1), (w_gate[0], w_up[0], router))
    (far,) = call(join_kernel, (far_up, far_low), [full], "join", (begun[2],))
    weights = (gate, up, router)
    begun = hidden_units([here, swap(here)], (0,), weights, begun, after=(far,))
    (hidden,) = hidden_units([far, swap(far)], (2,), weights, begun, end=True)
    (summed,), _ = reduce_blocks(hidden, *down)
    (expert_out,) = call(
        lambda s, x, o: from_slots_kernel(s, x, o),
        (slot.reshape(-1, 1), exchange(summed)),
        [((seq_len, width), BF16)],
        "from_slots",
    )
    return (attended, expert_out)


def solution(mesh):
    chips = mesh.shape["expert"] // 2
    fine = Mesh(mesh.devices.reshape(mesh.shape["dp"], chips, 2), ("dp", "x", "c"))
    e = ("x", "c")
    in_specs = (
        P("dp", e),
        P("dp", e),
        P("dp", e),
        P("dp", e),
        P(),
        P(e, None),
        P(),
        P("dp"),
        P("dp", None, e),
        P("dp", None, e),
        P("dp", e, None),
    )
    out_specs = (P("dp", e), P("dp", e))
    return jax.shard_map(shards, mesh=fine, in_specs=in_specs, out_specs=out_specs, check_vma=False)
```

```python
import functools
import math

import jax
import jax.numpy as jnp
from jax import lax
from jax.experimental import pallas as pl
from jax.experimental.pallas import tpu as pltpu
from jax.sharding import Mesh, PartitionSpec as P

HD = 128
EPSILON = 1e-05
BF16 = jnp.bfloat16
F32 = jnp.float32
ANY = pl.BlockSpec(memory_space=pl.ANY)
VMEM = pl.BlockSpec(memory_space=pltpu.VMEM)


def params(mib=20):
    return pltpu.CompilerParams(vmem_limit_bytes=mib * 1024 * 1024)


HOPS = (2, 1, -1, 0)
COST = pl.CostEstimate(flops=1024, bytes_accessed=1024, transcendentals=0)
TOKEN = jax.ShapeDtypeStruct((8, 128), F32)


def chip_at(hop):
    return lax.rem(lax.axis_index("x") + hop + 4, 4)


def column_copies(w_ref, targets, others, sems):
    core = lax.axis_index("c")
    width = targets[0].shape[1]
    copies = []
    for k, (hop, target) in enumerate(zip(HOPS, targets)):
        start = pl.multiple_of((2 * chip_at(hop) + (1 - core if others else core)) * width, 128)
        copy = pltpu.make_async_copy(w_ref.at[:, pl.ds(start, width)], target, sems.at[k])
        copy.start()
        copies.append(copy)
    return copies


def column_shape(w, width, n):
    return jax.ShapeDtypeStruct((n, w.shape[0], width), BF16)


def columns_kernel(w_ref, *refs):
    own_far_ref, own_rest_ref, far_ref, rest_ref, token_ref, sems, other_sems = refs[-7:]
    token_ref[...] = jnp.zeros_like(token_ref)
    copies = []
    for others, first, rest, used in ((True, far_ref, rest_ref, other_sems), (False, own_far_ref, own_rest_ref, sems)):
        targets = [first.at[0]] + [rest.at[k] for k in range(len(HOPS) - 1)]
        copies += column_copies(w_ref, targets, others, used)
    for copy in copies:
        copy.wait()


def columns(w, width, after=()):
    count = len(HOPS)
    return pl.pallas_call(
        columns_kernel,
        in_specs=[ANY] * (1 + len(after)),
        out_specs=[VMEM] * 5,
        out_shape=[column_shape(w, width, n) for n in (1, count - 1, 1, count - 1)] + [TOKEN],
        scratch_shapes=[pltpu.SemaphoreType.DMA((count,)), pltpu.SemaphoreType.DMA((count,))],
        cost_estimate=COST,
        compiler_params=params(),
        name="columns",
    )(w, *after)


def attend_kernel(halves, lengths_ref, q_ref, k_ref, v_ref, after_ref, out_ref):
    seq_len, head_width = q_ref.shape
    rows = seq_len // halves
    sequence = lax.axis_index("dp")
    for part in range(halves):
        first = part * rows
        span = first + rows
        row_at = lax.broadcasted_iota(jnp.int32, (rows, 1), 0) + first
        col_at = lax.broadcasted_iota(jnp.int32, (1, span), 1)
        bound = jnp.int32(0)
        row_doc = jnp.zeros((rows, 1), jnp.int32)
        col_doc = jnp.zeros((1, span), jnp.int32)
        for i in range(lengths_ref.shape[0]):
            bound = bound + lengths_ref[i, sequence]
            row_doc = row_doc + (row_at >= bound).astype(jnp.int32)
            col_doc = col_doc + (col_at >= bound).astype(jnp.int32)
        allowed = (row_doc == col_doc) & (col_at <= row_at)
        keys = k_ref[:span, :]
        values = v_ref[:span, :]
        for h in range(head_width // HD):
            cols = slice(h * HD, (h + 1) * HD)
            scores = lax.dot_general(
                q_ref[first:span, cols],
                keys,
                (((1,), (1,)), ((), ())),
                preferred_element_type=F32,
            )
            scores = jnp.where(allowed, scores, -1e30)
            scores = scores - jnp.max(scores, axis=1, keepdims=True)
            raised = jnp.exp2(scores * (math.log2(math.e) / math.sqrt(HD)))
            share = 1.0 / jnp.sum(raised, axis=1, keepdims=True)
            mixed = jnp.dot(raised.astype(BF16), values, preferred_element_type=F32) * share
            out_ref[first:span, cols] = mixed.astype(BF16)


def attend(lengths, queries, keys, values, after):
    return pl.pallas_call(
        functools.partial(attend_kernel, 2),
        out_shape=jax.ShapeDtypeStruct(queries.shape, BF16),
        in_specs=[pl.BlockSpec(memory_space=pltpu.SMEM), VMEM, VMEM, VMEM, VMEM],
        out_specs=VMEM,
        cost_estimate=COST,
        compiler_params=params(),
        name="attend",
    )(lengths.T, queries, keys, values, after)


def far_kernel(x_ref, xs_ref, w_ref, ws_ref, up_ref, low_ref):
    half = up_ref.shape[0]
    value = jnp.dot(x_ref[...], w_ref[0], preferred_element_type=F32)
    value = value + jnp.dot(xs_ref[...], ws_ref[0], preferred_element_type=F32)
    up_ref[...] = value[:half].astype(BF16)
    low_ref[...] = value[half:].astype(BF16)


def near_kernel(x_ref, xs_ref, w_ref, ws_ref, after_ref, near_low, near_up):
    half = near_up.shape[0]
    for k, rows, out_ref in ((1, slice(half, 2 * half), near_low), (2, slice(0, half), near_up)):
        value = jnp.dot(x_ref[rows, :], w_ref[k - 1], preferred_element_type=F32)
        value = value + jnp.dot(xs_ref[rows, :], ws_ref[k - 1], preferred_element_type=F32)
        out_ref[...] = value.astype(BF16)


def rest_kernel(x_ref, xs_ref, w_ref, ws_ref, after_ref, next_up, next_low, own_ref):
    half = next_up.shape[0]
    for k, rows, out_ref in (
        (1, slice(0, half), next_up),
        (2, slice(half, 2 * half), next_low),
        (3, slice(0, 2 * half), own_ref),
    ):
        value = jnp.dot(x_ref[rows, :], w_ref[k - 1], preferred_element_type=F32)
        out_ref[...] = value + jnp.dot(xs_ref[rows, :], ws_ref[k - 1], preferred_element_type=F32)


def next_kernel(next_up, next_low, far_up, far_low, up_ref, low_ref):
    up_ref[...] = (next_up[...] + far_up[...].astype(F32)).astype(BF16)
    low_ref[...] = (next_low[...] + far_low[...].astype(F32)).astype(BF16)


def own_kernel(attention, count, own_ref, *refs):
    arrived = refs[:4]
    half = arrived[0].shape[0]
    for lower in range(2):
        rows = slice(lower * half, (lower + 1) * half)
        value = own_ref[rows, :]
        for ref in arrived[2 * lower : 2 * lower + 2]:
            value = value + ref[...].astype(F32)
        if attention:
            residual_ref, slot_ref = refs[4:6]
            out_ref, slots_ref = refs[6 + count :]
            value = value + residual_ref[rows, :].astype(F32)
        else:
            out_ref = refs[4 + count]
        out_ref[rows, :] = value.astype(BF16)
    if attention:
        places = lax.broadcasted_iota(jnp.int32, (slots_ref.shape[0], 1), 0)
        pick = (places == slot_ref[...]).astype(F32).astype(BF16)
        slots_ref[...] = jnp.dot(pick, out_ref[...], preferred_element_type=F32).astype(BF16)


def call(kernel, inputs, outs, name, after=()):
    return pl.pallas_call(
        kernel,
        in_specs=[VMEM] * len(inputs) + [ANY] * len(after),
        out_specs=[VMEM] * len(outs),
        out_shape=[jax.ShapeDtypeStruct(shape, dtype) for shape, dtype in outs],
        cost_estimate=COST,
        compiler_params=params(),
        name=name,
    )(*inputs, *after)


def swap(x):
    return lax.ppermute(x, "c", [(0, 1), (1, 0)])


def shift(x, by):
    size = lax.axis_size("x")
    return lax.ppermute(x, "x", [(i, (i + by) % size) for i in range(size)])


def reduce_blocks(x, w_far, w_rest, other_far, other_rest, attention=(), slots=None, middle=None):
    xs = swap(x)
    rows, depth = x.shape
    width = w_far.shape[2]
    half = ((rows // 2, width), BF16)
    half_f32 = ((rows // 2, width), F32)
    far = call(far_kernel, (x, xs, w_far, other_far), [half] * 2, "far_blocks")
    far_up, far_low = shift(far[0], 1), shift(far[1], -1)
    near = call(
        near_kernel,
        (x, xs, w_rest, other_rest, far[0]),
        [half] * 2,
        "near_blocks",
    )
    near_low, near_up = shift(near[0], 1), shift(near[1], -1)
    next_up, next_low, own = call(
        rest_kernel,
        (x, xs, w_rest, other_rest, near[0]),
        [half_f32, half_f32, ((rows, width), F32)],
        "rest_blocks",
    )
    last = call(next_kernel, (next_up, next_low, far_up, far_low), [half] * 2, "next_blocks")
    last_up, last_low = shift(last[0], 1), shift(last[1], -1)
    inputs = [own, near_up, last_up, near_low, last_low]
    outs = [((rows, width), BF16)]
    if attention:
        inputs += attention
        outs.append(((slots, width), BF16))
    between = middle(last[0]) if middle else ()
    kernel = functools.partial(own_kernel, bool(attention), len(between[-1:]))
    return call(kernel, inputs, outs, "own_block", between[-1:]), between


def hidden_kernel(hops, begin, end, features, count, *refs):
    shards = 2 * len(hops)
    x_refs = refs[:shards]
    wg_ref, wu_ref, wr_ref = refs[shards : shards + 3]
    rest = refs[shards + 3 :]
    depth = 2 * x_refs[0].shape[1]
    first_core = lax.axis_index("c") == 0
    sums = None
    if not begin:
        sums, rest = [ref[...] for ref in rest[:4]], rest[4:]
    rest = rest[count:]
    for k, hop in enumerate(hops):
        mine, other = x_refs[2 * k][...], x_refs[2 * k + 1][...]
        x = jnp.concatenate(
            [jnp.where(first_core, mine, other), jnp.where(first_core, other, mine)], axis=1
        )
        start = pl.multiple_of(chip_at(hop) * depth, 128)
        at = 0 if hop == 0 else depth
        rows = pl.ds(start, depth) if begin else slice(at, at + depth)
        wide = x.astype(F32)
        terms = (
            jnp.dot(x, wg_ref[rows, :], preferred_element_type=F32),
            jnp.dot(x, wu_ref[rows, :], preferred_element_type=F32),
            jnp.sum(wide * wide, axis=1, keepdims=True),
            jnp.sum(wide * wr_ref[:, pl.ds(start, depth)], axis=1, keepdims=True),
        )
        sums = terms if sums is None else [a + b for a, b in zip(sums, terms)]
    if not end:
        for ref, value in zip(rest, sums):
            ref[...] = value
        if begin:
            for i, hop in enumerate((0, 2)):
                rows = pl.ds(pl.multiple_of(chip_at(hop) * depth, 128), depth)
                rest[4][i * depth : (i + 1) * depth, :] = wg_ref[rows, :]
                rest[5][i * depth : (i + 1) * depth, :] = wu_ref[rows, :]
        return
    gate, up, squares, logits = sums
    inverse = lax.rsqrt(squares / features + EPSILON)
    scale = inverse / (1.0 + jnp.exp(-logits * inverse))
    gate = gate * scale
    rest[0][...] = (gate / (1.0 + jnp.exp(-gate)) * (up * scale)).astype(BF16)


def hidden_units(shards, hops, weights, begun=(), end=False, after=()):
    rows, width = shards[0].shape
    features, units = weights[2].shape[1], weights[0].shape[1]
    if end:
        outs = [((rows, units), BF16)]
    else:
        outs = [((rows, n), F32) for n in (units, units, 1, 1)]
        outs += [] if begun else [((4 * width, units), BF16)] * 2
    kernel = functools.partial(hidden_kernel, hops, not begun, end, features, len(after))
    return call(kernel, (*shards, *weights, *begun), outs, "hidden", after)


def halves_kernel(behind_ref, ahead_ref, up_ref, low_ref):
    half = up_ref.shape[0]
    up_ref[...] = behind_ref[:half, :]
    low_ref[...] = ahead_ref[half:, :]


def join_kernel(up_ref, low_ref, *refs):
    half = up_ref.shape[0]
    refs[-1][:half, :] = up_ref[...]
    refs[-1][half:, :] = low_ref[...]


def from_slots_kernel(slot_ref, x_ref, out_ref):
    places = lax.broadcasted_iota(jnp.int32, (1, x_ref.shape[0]), 1)
    pick = (slot_ref[...] == places).astype(F32).astype(BF16)
    out_ref[...] = jnp.dot(pick, x_ref[...], preferred_element_type=F32).astype(BF16)


def shards(
    residual, queries, keys, values, lengths, w_out, w_router, expert_ids, w_gate, w_up, w_down
):
    seq_len = queries.shape[0]
    width = residual.shape[1]
    dp_count = lax.axis_size("dp")
    expert_count = w_router.shape[1]
    capacity = 3 * seq_len // (2 * expert_count)
    slots = expert_count * capacity

    same = expert_ids[:, None] == expert_ids[None, :]
    token_at = jnp.arange(seq_len, dtype=jnp.int32)
    rank = jnp.sum((same & (token_at[None, :] < token_at[:, None])).astype(jnp.int32), axis=1)
    slot = expert_ids * capacity + rank

    router = lax.dynamic_index_in_dim(w_router.astype(F32).T, lax.axis_index("dp"), 0)

    w_far, w_rest, other_far, other_rest, token = columns(w_out, width)
    context = attend(lengths, queries, keys, values, token)

    (attended, outgoing), (*down, _) = reduce_blocks(
        context,
        w_far,
        w_rest,
        swap(other_far),
        swap(other_rest),
        [residual, slot.reshape(1, -1)],
        slots,
        lambda done: columns(w_down[0], width, (done,)),
    )
    down[2], down[3] = swap(down[2]), swap(down[3])

    def exchange(x):
        x = x.reshape(dp_count, slots // dp_count, width)
        return lax.all_to_all(x, "dp", split_axis=0, concat_axis=0, tiled=True).reshape(slots, width)

    here = exchange(outgoing)
    behind, ahead = shift(here, 1), shift(here, -1)
    half, full = ((slots // 2, width), BF16), ((slots, width), BF16)
    behind_up, ahead_low = call(halves_kernel, (behind, ahead), [half] * 2, "halves")
    far_up, far_low = shift(behind_up, 1), shift(ahead_low, -1)
    beside = [behind, swap(behind), ahead, swap(ahead)]
    *begun, gate, up = hidden_units(beside, (-1, 1), (w_gate[0], w_up[0], router))
    (far,) = call(join_kernel, (far_up, far_low), [full], "join", (begun[2], down[2]))
    weights = (gate, up, router)
    begun = hidden_units([here, swap(here)], (0,), weights, begun, after=(far,))
    (hidden,) = hidden_units([far, swap(far)], (2,), weights, begun, end=True)
    (summed,), _ = reduce_blocks(hidden, *down)
    (expert_out,) = call(
        lambda s, x, o: from_slots_kernel(s, x, o),
        (slot.reshape(-1, 1), exchange(summed)),
        [((seq_len, width), BF16)],
        "from_slots",
    )
    return (attended, expert_out)


def solution(mesh):
    chips = mesh.shape["expert"] // 2
    fine = Mesh(mesh.devices.reshape(mesh.shape["dp"], chips, 2), ("dp", "x", "c"))
    e = ("x", "c")
    in_specs = (
        P("dp", e),
        P("dp", e),
        P("dp", e),
        P("dp", e),
        P(),
        P(e, None),
        P(),
        P("dp"),
        P("dp", None, e),
        P("dp", None, e),
        P("dp", e, None),
    )
    out_specs = (P("dp", e), P("dp", e))
    return jax.shard_map(shards, mesh=fine, in_specs=in_specs, out_specs=out_specs, check_vma=False)
```
